256 devices in a mesh: batch: 256 (over y, x, z, core).
Axes of the slice: x: 4, y: 4, z: 8, core: 2. Of those that a mesh axis runs over, the one named last changes fastest.
Arguments:
- image_emb: float32 [98304, 1152], P('batch'), may hold values from -0.1875 to 0.1875
- text_emb: float32 [98304, 1152], P('batch'), may hold values from -0.1875 to 0.1875
- log_scale: float32 [1], replicated, may hold values from 1.6 to 2.7
- logit_bias: float32 [1], replicated, may hold values from -4 to -1
Outputs:
- image_grad: float32 [98304, 1152], P('batch')
- text_grad: float32 [98304, 1152], P('batch')
The draws below stay inside these ranges and needn't reach their ends.
All inputs are finite; a program needn't handle non-finite values.
Results may differ from the reference program's by a relative error of at most 0.0001.
Values sent between devices are 32-bit elements; how exact they have to be, the bound alone decides.
No kernel may reach another device: no remote copies, remote signals or barrier semaphores. Data moves between devices by JAX's collectives and lax.ppermute only.
A program may use at most 64 MiB of HBM per device.

```python
import jax
import jax.numpy as jnp
from jax import lax

D = 1152
ROWS = 384
STEPS = 3
TOTAL = 98304
N_BATCH = 256


def level_of(stream_key, shape, pieces, low, high):
    level, own = 1.0, jax.random.fold_in(stream_key, 6)
    for axis_at, blocks in pieces:
        heights = jnp.exp(jax.random.uniform(jax.random.fold_in(own, axis_at), (blocks,), jnp.float32, low / len(pieces), high / len(pieces)))
        level = level * jnp.repeat(heights, shape[axis_at] // blocks).reshape([-1 if axis == axis_at else 1 for axis in range(len(shape))])
    return level


def noise(stream_key, dims, scale, most, pieces=(), kind=jnp.bfloat16):
    entries = scale * jax.random.normal(stream_key, dims, jnp.float32)
    if pieces:
        entries = entries * level_of(stream_key, dims, pieces, -0.22, 0.18)
    return jnp.clip(entries, -most, most).astype(kind)


def setup_inputs(seed: int = 0) -> dict:
    keys = jax.random.split(jax.random.key(seed), 5)
    image_emb = noise(keys[0], (TOTAL, D), D ** -0.5, 0.1875, ((0, 256),), jnp.float32)
    text_emb = noise(keys[1], (TOTAL, D), D ** -0.5, 0.1875, ((0, 256),), jnp.float32)
    log_scale = jnp.clip(jax.random.uniform(keys[2], (1,), jnp.float32, 1.6, 2.7), 1.6, 2.7)
    logit_bias = jnp.clip(jax.random.uniform(keys[3], (1,), jnp.float32, -4.0, -1.0), -4.0, -1.0)
    return {"image_emb": image_emb, "text_emb": text_emb, "log_scale": log_scale, "logit_bias": logit_bias}


epsilon = 1e-06

def normalize(values):
    norms = jnp.sqrt(lax.optimization_barrier(jnp.sum(values * values, axis=-1, keepdims=True)) + epsilon)
    return (values / norms, norms)

def reference(image_emb, text_emb, log_scale, logit_bias):
    temper = jnp.exp(log_scale[0])
    offset_bias = logit_bias[0]
    img_unit, img_norm = normalize(image_emb)
    txt_unit, txt_norm = normalize(text_emb)
    img_blocks = img_unit.reshape(N_BATCH, ROWS, D)
    txt_blocks = txt_unit.reshape(N_BATCH, ROWS, D)
    identity = jnp.eye(ROWS, dtype=jnp.float32)
    img_acc = jnp.zeros((N_BATCH, ROWS, D), jnp.float32)
    txt_acc = jnp.zeros((N_BATCH, ROWS, D), jnp.float32)
    for offset in range(-STEPS, STEPS + 1):
        rolled = jnp.roll(txt_blocks, offset, axis=0)
        logits = temper * jnp.einsum('nbd,ncd->nbc', img_blocks, rolled, precision=lax.Precision.HIGHEST) + offset_bias
        weights = jax.nn.sigmoid(logits)
        if offset == 0:
            weights = weights - identity
        img_acc = img_acc + temper * jnp.einsum('nbc,ncd->nbd', weights, rolled, precision=lax.Precision.HIGHEST)
        back = temper * jnp.einsum('nbc,nbd->ncd', weights, img_blocks, precision=lax.Precision.HIGHEST)
        txt_acc = txt_acc + jnp.roll(back, -offset, axis=0)
    img_acc = img_acc.reshape(TOTAL, D)
    txt_acc = txt_acc.reshape(TOTAL, D)
    image_grad = (img_acc - img_unit * lax.optimization_barrier(jnp.sum(img_acc * img_unit, axis=-1, keepdims=True))) / img_norm
    text_grad = (txt_acc - txt_unit * lax.optimization_barrier(jnp.sum(txt_acc * txt_unit, axis=-1, keepdims=True))) / txt_norm
    return (image_grad, text_grad)
```

```python
import jax
import jax.numpy as jnp
from jax import lax
from jax.sharding import PartitionSpec as P

EPSILON = 1e-06


def outward(i):
    return i + 2 if i % 2 else i - 2


def inward(i):
    return i - 2 if i % 2 else i + 2


def relay(i):
    return i + 1 if i % 2 else i - 1


def sibling(i):
    return i ^ 1


def sent(value, where):
    count = lax.axis_size("batch")
    pairs = [(source, where(source) % count) for source in range(count)]
    return lax.ppermute(value, "batch", pairs)


def contract(first_rows, other_rows, first_dim, other_dim):
    return lax.dot_general(
        first_rows,
        other_rows,
        (((first_dim,), (other_dim,)), ((), ())),
        precision=lax.Precision.HIGH,
        preferred_element_type=jnp.float32,
    )


def norm_of(values):
    return jnp.sqrt(jnp.sum(values * values, axis=-1, keepdims=True) + EPSILON)


def guest_term(own_unit, guest, temper, offset_bias):
    scale = (temper / norm_of(guest)).reshape(1, -1)
    weights = jax.nn.sigmoid(contract(own_unit, guest, 1, 1) * scale + offset_bias)
    return contract(weights * scale, guest, 1, 0)


def unnormalize(unit_grad, unit_rows, norms):
    return (unit_grad - unit_rows * jnp.sum(unit_grad * unit_rows, axis=-1, keepdims=True)) / norms


def body(image_emb, text_emb, log_scale, logit_bias):
    temper = jnp.exp(log_scale[0])
    offset_bias = logit_bias[0]
    own = (image_emb, text_emb)
    out_far = [sent(value, outward) for value in own]
    in_far = [sent(value, inward) for value in own]
    near = [sent(value, sibling) for value in own]
    farthest = [sent(value, relay) for value in out_far]
    out_near = [sent(value, sibling) for value in out_far]
    in_near = [sent(value, sibling) for value in in_far]
    norms = [norm_of(value) for value in own]
    units = [value / norm for value, norm in zip(own, norms)]
    logits = temper * contract(units[0], units[1], 1, 1) + offset_bias
    weights = jax.nn.sigmoid(logits) - jnp.eye(logits.shape[0], dtype=jnp.float32)
    grads = [temper * contract(weights, units[1], 1, 0), temper * contract(weights, units[0], 0, 0)]
    for guests in (near, out_far, in_far, out_near, in_near, farthest):
        for kind in (0, 1):
            grads[1 - kind] = grads[1 - kind] + guest_term(units[1 - kind], guests[kind], temper, offset_bias)
    return tuple(unnormalize(grad, unit, norm) for grad, unit, norm in zip(grads, units, norms))


def solution(mesh):
    placed = (P("batch", None), P("batch", None), P(), P())
    return jax.shard_map(
        body,
        mesh=mesh,
        in_specs=placed,
        out_specs=(P("batch", None), P("batch", None)),
        check_vma=False,
    )
```

```python
import functools

import jax
import jax.numpy as jnp
from jax import lax
from jax.experimental import pallas as pl
from jax.experimental.pallas import tpu as pltpu
from jax.sharding import PartitionSpec as P

EPSILON = 1e-06
FLOPS = 60
COST = 560000
CUT = 256
VMEM_LIMIT = 10 * 1024 * 1024
STRIP = 32


def outward(i):
    return i + 2 if i % 2 else i - 2


def inward(i):
    return i - 2 if i % 2 else i + 2


def relay(i):
    return i + 1 if i % 2 else i - 1


def sibling(i):
    return i ^ 1


def sent(value, where, name):
    count = lax.axis_size("batch")
    pairs = [(source, where(source) % count) for source in range(count)]
    with jax.named_scope(name):
        return lax.ppermute(value, "batch", pairs)


def halves(values):
    high = values.astype(jnp.bfloat16)
    return high, (values - high.astype(jnp.float32)).astype(jnp.bfloat16)


def dot(first, other, other_dim):
    return lax.dot_general(first, other, (((1,), (other_dim,)), ((), ())), preferred_element_type=jnp.float32)


def row_dots(unit, stack, rows):
    own = unit.shape[0] // 2
    wide = dot(unit[:own, :], stack[: 2 * rows, :], 1)
    return wide[:, :rows] + (wide[:, rows:] + dot(unit[own:, :], stack[:rows, :], 1))


def norm_of(values):
    return jnp.sqrt(jnp.sum(values * values, axis=-1, keepdims=True) + EPSILON)


def own_kernel(scalars, img, txt, img_unit, txt_unit, img_grad, txt_grad, img_along, txt_along, img_norm, txt_norm):
    temper, offset_bias = scalars[0], scalars[1]
    rows = img.shape[0]
    for source, unit, norms in ((img, img_unit, img_norm), (txt, txt_unit, txt_norm)):
        for start in range(0, rows, STRIP):
            values = source[start : start + STRIP, :]
            norm = norm_of(values)
            norms[start : start + STRIP, :] = norm
            unit[start : start + STRIP, :], unit[rows + start : rows + start + STRIP, :] = halves(values * (1.0 / norm))
    dots = row_dots(img_unit, txt_unit, rows)
    diagonal = lax.broadcasted_iota(jnp.int32, dots.shape, 0) == lax.broadcasted_iota(jnp.int32, dots.shape, 1)
    weights = temper * (jax.nn.sigmoid(temper * dots + offset_bias) - jnp.where(diagonal, 1.0, 0.0))
    turned = jnp.transpose(weights)
    img_along[...] = jnp.sum(weights * dots, axis=1, keepdims=True)
    txt_along[...] = jnp.sum(turned * jnp.transpose(dots), axis=1, keepdims=True)
    for grad, matrix, unit in ((img_grad, weights, txt_unit), (txt_grad, turned, img_unit)):
        high, low = halves(matrix)
        grad[...] = dot(jnp.concatenate([high, high], axis=1), unit[...], 0) + dot(low, unit[:rows, :], 0)


def guest_sums(scalars, unit, guest, along, stack, squares):
    rows = guest.shape[0]
    for start in range(0, rows, STRIP):
        values = guest[start : start + STRIP, :]
        high, low = halves(values)
        stack[start : start + STRIP, :] = high
        stack[rows + start : rows + start + STRIP, :] = low
        stack[2 * rows + start : 2 * rows + start + STRIP, :] = high
        total = jnp.sum(values * values, axis=-1, keepdims=True)
        squares[start : start + STRIP, :] = jnp.broadcast_to(total, (STRIP, squares.shape[1]))
    scale = scalars[0] / jnp.sqrt(jnp.transpose(squares[...])[0:1, :] + EPSILON)
    dots = row_dots(unit, stack, rows)
    weights = jax.nn.sigmoid(dots * scale + scalars[1]) * scale
    high, low = halves(weights)
    term = dot(jnp.concatenate([high, high, low], axis=1), stack[...], 0)
    return along[...] + jnp.sum(weights * dots, axis=1, keepdims=True), term


def guest_kernel(scalars, unit, guest, grad, along, grad_out, along_out, stack, squares):
    along_out[...], term = guest_sums(scalars, unit, guest, along, stack, squares)
    grad_out[...] = grad[...] + term


def last_kernel(scalars, unit, guest, grad, along, own, norm, out, stack, squares):
    along, term = guest_sums(scalars, unit, guest, along, stack, squares)
    inverse = 1.0 / norm[...]
    out[...] = (grad[...] + term) * inverse - own[...] * (along * inverse * inverse)


def call(kernel, outs, aliases, *operands):
    rows = operands[2].shape[0]
    width = operands[2].shape[1]
    in_specs = [pl.BlockSpec(memory_space=pltpu.SMEM)] + [pl.BlockSpec(memory_space=pltpu.VMEM)] * (len(operands) - 1)
    scratch = [] if kernel is own_kernel else [pltpu.VMEM((3 * rows, width), jnp.bfloat16), pltpu.VMEM((rows, 128), jnp.float32)]
    return pl.pallas_call(
        kernel,
        out_shape=[jax.ShapeDtypeStruct(*out) for out in outs],
        in_specs=in_specs,
        out_specs=[pl.BlockSpec(memory_space=pltpu.VMEM)] * len(outs),
        scratch_shapes=scratch,
        input_output_aliases=aliases,
        cost_estimate=pl.CostEstimate(flops=FLOPS * operands[1].size * rows, bytes_accessed=COST * rows, transcendentals=0),
        compiler_params=pltpu.CompilerParams(vmem_limit_bytes=VMEM_LIMIT),
    )(*operands)


def body(image_emb, text_emb, log_scale, logit_bias):
    scalars = jnp.concatenate([jnp.exp(log_scale), logit_bias])
    own = (image_emb, text_emb)
    near = [sent(value, sibling, name) for value, name in zip(own, ("near_image", "near_text"))]
    out_far = [sent(value, outward, name) for value, name in zip(own, ("outward_image", "outward_text"))]
    in_far = [sent(image_emb, inward, "inward_image"), None]
    rows, width = image_emb.shape
    full, pair, column = ((rows, width), jnp.float32), ((2 * rows, width), jnp.bfloat16), ((rows, 1), jnp.float32)
    results = call(own_kernel, [pair] * 2 + [full] * 2 + [column] * 4, {}, scalars, *own)
    units, grads, alongs, norms = results[0:2], list(results[2:4]), list(results[4:6]), results[6:8]

    def gated(*values):
        *values, grads[0], grads[1] = lax.optimization_barrier((*values, *grads))
        return values

    def add(kind, guest):
        (guest,) = gated(guest)
        side = 1 - kind
        grads[side], alongs[side] = call(
            guest_kernel, [full, column], {3: 0, 4: 1}, scalars, units[side], guest, grads[side], alongs[side]
        )

    def finish(kind, guest):
        (guest,) = gated(guest)
        side = 1 - kind
        return call(last_kernel, [full], {}, scalars, units[side], guest, grads[side], alongs[side], own[side], norms[side])[0]

    in_far[1] = sent(text_emb, inward, "inward_text")
    add(0, near[0])
    add(1, near[1])
    out_far[0], in_far[0] = gated(out_far[0], in_far[0])
    farthest = [sent(out_far[0], relay, "relay_image"), None]
    out_near = [sent(out_far[0], sibling, "outward_image_near"), None]
    in_near = [sent(in_far[0], sibling, "inward_image_near"), None]
    add(0, out_far[0])
    add(0, in_far[0])
    add(0, out_near[0])
    add(0, in_near[0])
    (out_far[1],) = gated(out_far[1])
    farthest[1] = sent(out_far[1], relay, "relay_text")
    out_near[1] = sent(out_far[1], sibling, "outward_text_near")
    add(1, out_far[1])
    add(1, out_near[1])
    (in_far[1],) = gated(in_far[1])
    in_near[1] = sent(in_far[1], sibling, "inward_text_near")
    add(1, in_far[1])
    add(1, in_near[1])
    text_grad = finish(0, farthest[0])
    last, text_grad = lax.optimization_barrier((farthest[1], text_grad))
    image_grad = finish(1, last)
    return image_grad, text_grad


def solution(mesh):
    placed = (P("batch", None), P("batch", None), P(), P())
    return jax.shard_map(
        body,
        mesh=mesh,
        in_specs=placed,
        out_specs=(P("batch", None), P("batch", None)),
        check_vma=False,
    )
```

```python
import functools

import jax
import jax.numpy as jnp
from jax import lax
from jax.experimental import pallas as pl
from jax.experimental.pallas import tpu as pltpu
from jax.sharding import PartitionSpec as P

EPSILON = 1e-06
FLOPS = 60
COST = 560000
CUT = 256
PARTS = 3
VMEM_LIMIT = 10 * 1024 * 1024
STRIP = 32


def outward(i):
    return i + 2 if i % 2 else i - 2


def inward(i):
    return i - 2 if i % 2 else i + 2


def relay(i):
    return i + 1 if i % 2 else i - 1


def sibling(i):
    return i ^ 1


def sent(value, where, name):
    count = lax.axis_size("batch")
    pairs = [(source, where(source) % count) for source in range(count)]
    with jax.named_scope(name):
        return lax.ppermute(value, "batch", pairs)


def halves(values):
    high = values.astype(jnp.bfloat16)
    return high, (values - high.astype(jnp.float32)).astype(jnp.bfloat16)


def dot(first, other, other_dim):
    return lax.dot_general(first, other, (((1,), (other_dim,)), ((), ())), preferred_element_type=jnp.float32)


def row_dots(unit, stack, rows):
    own = unit.shape[0] // 2
    wide = dot(unit[:own, :], stack[: 2 * rows, :], 1)
    return wide[:, :rows] + (wide[:, rows:] + dot(unit[own:, :], stack[:rows, :], 1))


def norm_of(values):
    return jnp.sqrt(jnp.sum(values * values, axis=-1, keepdims=True) + EPSILON)


def own_kernel(scalars, img, txt, img_unit, txt_unit, img_grad, txt_grad, img_along, txt_along, img_norm, txt_norm):
    temper, offset_bias = scalars[0], scalars[1]
    rows = img.shape[0]
    for source, unit, norms in ((img, img_unit, img_norm), (txt, txt_unit, txt_norm)):
        for start in range(0, rows, STRIP):
            values = source[start : start + STRIP, :]
            norm = norm_of(values)
            norms[start : start + STRIP, :] = norm
            unit[start : start + STRIP, :], unit[rows + start : rows + start + STRIP, :] = halves(values * (1.0 / norm))
    dots = row_dots(img_unit, txt_unit, rows)
    diagonal = lax.broadcasted_iota(jnp.int32, dots.shape, 0) == lax.broadcasted_iota(jnp.int32, dots.shape, 1)
    weights = temper * (jax.nn.sigmoid(temper * dots + offset_bias) - jnp.where(diagonal, 1.0, 0.0))
    turned = jnp.transpose(weights)
    img_along[...] = jnp.sum(weights * dots, axis=1, keepdims=True)
    txt_along[...] = jnp.sum(turned * jnp.transpose(dots), axis=1, keepdims=True)
    for grad, matrix, unit in ((img_grad, weights, txt_unit), (txt_grad, turned, img_unit)):
        high, low = halves(matrix)
        grad[...] = dot(jnp.concatenate([high, high], axis=1), unit[...], 0) + dot(low, unit[:rows, :], 0)


def guest_weights(scalars, unit, guest, along, stack, squares):
    rows = guest.shape[0]
    for start in range(0, rows, STRIP):
        values = guest[start : start + STRIP, :]
        high, low = halves(values)
        stack[start : start + STRIP, :] = high
        stack[rows + start : rows + start + STRIP, :] = low
        stack[2 * rows + start : 2 * rows + start + STRIP, :] = high
        total = jnp.sum(values * values, axis=-1, keepdims=True)
        squares[start : start + STRIP, :] = jnp.broadcast_to(total, (STRIP, squares.shape[1]))
    scale = scalars[0] / jnp.sqrt(jnp.transpose(squares[...])[0:1, :] + EPSILON)
    dots = row_dots(unit, stack, rows)
    weights = jax.nn.sigmoid(dots * scale + scalars[1]) * scale
    high, low = halves(weights)
    return along[...] + jnp.sum(weights * dots, axis=1, keepdims=True), jnp.concatenate([high, high, low], axis=1)


def guest_kernel(scalars, unit, guest, grad, along, grad_out, along_out, stack, squares):
    along_out[...], weights = guest_weights(scalars, unit, guest, along, stack, squares)
    grad_out[...] = grad[...] + dot(weights, stack[...], 0)


def last_kernel(scalars, unit, guest, grad, along, own, norm, out, stack, squares, result, sems):
    along, weights = guest_weights(scalars, unit, guest, along, stack, squares)
    inverse = 1.0 / norm[...]
    along = along * inverse * inverse
    copies = []
    for part in range(PARTS):
        width = out.shape[1] // PARTS
        span = slice(part * width, (part + 1) * width)
        result[:, span] = (grad[:, span] + dot(weights, stack[:, span], 0)) * inverse - own[:, span] * along
        copies.append(pltpu.make_async_copy(result.at[:, span], out.at[:, span], sems.at[part]))
        copies[-1].start()
    for copy in copies:
        copy.wait()


def call(kernel, outs, aliases, *operands):
    rows, width = operands[2].shape
    in_specs = [pl.BlockSpec(memory_space=pltpu.SMEM)] + [pl.BlockSpec(memory_space=pltpu.VMEM)] * (len(operands) - 1)
    out_space, scratch = pltpu.VMEM, []
    if kernel is not own_kernel:
        scratch = [pltpu.VMEM((3 * rows, width), jnp.bfloat16), pltpu.VMEM((rows, 128), jnp.float32)]
    if kernel is last_kernel:
        out_space = pl.ANY
        scratch += [pltpu.VMEM(*outs[0]), pltpu.SemaphoreType.DMA((PARTS,))]
    return pl.pallas_call(
        kernel,
        out_shape=[jax.ShapeDtypeStruct(*out) for out in outs],
        in_specs=in_specs,
        out_specs=[pl.BlockSpec(memory_space=out_space)] * len(outs),
        scratch_shapes=scratch,
        input_output_aliases=aliases,
        cost_estimate=pl.CostEstimate(flops=FLOPS * operands[1].size * rows, bytes_accessed=COST * rows, transcendentals=0),
        compiler_params=pltpu.CompilerParams(vmem_limit_bytes=VMEM_LIMIT),
    )(*operands)


def body(image_emb, text_emb, log_scale, logit_bias):
    scalars = jnp.concatenate([jnp.exp(log_scale), logit_bias])
    own = (image_emb, text_emb)
    near = [sent(value, sibling, name) for value, name in zip(own, ("near_image", "near_text"))]
    out_far = [sent(value, outward, name) for value, name in zip(own, ("outward_image", "outward_text"))]
    in_far = [sent(image_emb, inward, "inward_image"), None]
    rows, width = image_emb.shape
    full, pair, column = ((rows, width), jnp.float32), ((2 * rows, width), jnp.bfloat16), ((rows, 1), jnp.float32)
    results = call(own_kernel, [pair] * 2 + [full] * 2 + [column] * 4, {}, scalars, *own)
    units, grads, alongs, norms = results[0:2], list(results[2:4]), list(results[4:6]), results[6:8]

    def gated(*values):
        *values, grads[0], grads[1] = lax.optimization_barrier((*values, *grads))
        return values

    def add(kind, guest):
        (guest,) = gated(guest)
        side = 1 - kind
        grads[side], alongs[side] = call(
            guest_kernel, [full, column], {3: 0, 4: 1}, scalars, units[side], guest, grads[side], alongs[side]
        )

    def finish(kind, guest):
        (guest,) = gated(guest)
        side = 1 - kind
        return call(last_kernel, [full], {}, scalars, units[side], guest, grads[side], alongs[side], own[side], norms[side])[0]

    in_far[1] = sent(text_emb, inward, "inward_text")
    add(0, near[0])
    add(1, near[1])
    out_far[0], in_far[0] = gated(out_far[0], in_far[0])
    farthest = [sent(out_far[0], relay, "relay_image"), None]
    out_near = [sent(out_far[0], sibling, "outward_image_near"), None]
    in_near = [sent(in_far[0], sibling, "inward_image_near"), None]
    add(0, out_far[0])
    add(0, in_far[0])
    add(0, out_near[0])
    add(0, in_near[0])
    (out_far[1],) = gated(out_far[1])
    farthest[1] = [sent(part, relay, "relay_text") for part in (out_far[1][:CUT], out_far[1][CUT:])]
    out_near[1] = sent(out_far[1], sibling, "outward_text_near")
    add(1, out_far[1])
    add(1, out_near[1])
    (in_far[1],) = gated(in_far[1])
    in_near[1] = sent(in_far[1], sibling, "inward_text_near")
    add(1, in_far[1])
    add(1, in_near[1])
    text_grad = finish(0, farthest[0])
    part, text_grad = lax.optimization_barrier((farthest[1][0], text_grad))
    add(1, part)
    image_grad = finish(1, farthest[1][1])
    return image_grad, text_grad


def solution(mesh):
    placed = (P("batch", None), P("batch", None), P(), P())
    return jax.shard_map(
        body,
        mesh=mesh,
        in_specs=placed,
        out_specs=(P("batch", None), P("batch", None)),
        check_vma=False,
    )
```

```python
import functools

import jax
import jax.numpy as jnp
from jax import lax
from jax.experimental import pallas as pl
from jax.experimental.pallas import tpu as pltpu
from jax.sharding import PartitionSpec as P

EPSILON = 1e-06
FLOPS = 60
NEAR_CUT = 128
COST = 560000
CUT = 256
PARTS = 3
VMEM_LIMIT = 10 * 1024 * 1024
STRIP = 32


def outward(i):
    return i + 2 if i % 2 else i - 2


def inward(i):
    return i - 2 if i % 2 else i + 2


def relay(i):
    return i + 1 if i % 2 else i - 1


def sibling(i):
    return i ^ 1


def sent(value, where, name):
    count = lax.axis_size("batch")
    pairs = [(source, where(source) % count) for source in range(count)]
    with jax.named_scope(name):
        return lax.ppermute(value, "batch", pairs)


def halves(values):
    high = values.astype(jnp.bfloat16)
    return high, (values - high.astype(jnp.float32)).astype(jnp.bfloat16)


def dot(first, other, other_dim):
    return lax.dot_general(first, other, (((1,), (other_dim,)), ((), ())), preferred_element_type=jnp.float32)


def row_dots(unit, stack, rows):
    own = unit.shape[0] // 2
    wide = dot(unit[:own, :], stack[: 2 * rows, :], 1)
    return wide[:, :rows] + (wide[:, rows:] + dot(unit[own:, :], stack[:rows, :], 1))


def norm_of(values):
    return jnp.sqrt(jnp.sum(values * values, axis=-1, keepdims=True) + EPSILON)


def own_kernel(scalars, img, txt, img_unit, txt_unit, img_grad, txt_grad, img_along, txt_along, img_norm, txt_norm):
    temper, offset_bias = scalars[0], scalars[1]
    rows = img.shape[0]
    for source, unit, norms in ((img, img_unit, img_norm), (txt, txt_unit, txt_norm)):
        for start in range(0, rows, STRIP):
            values = source[start : start + STRIP, :]
            norm = norm_of(values)
            norms[start : start + STRIP, :] = norm
            unit[start : start + STRIP, :], unit[rows + start : rows + start + STRIP, :] = halves(values * (1.0 / norm))
    dots = row_dots(img_unit, txt_unit, rows)
    diagonal = lax.broadcasted_iota(jnp.int32, dots.shape, 0) == lax.broadcasted_iota(jnp.int32, dots.shape, 1)
    weights = temper * (jax.nn.sigmoid(temper * dots + offset_bias) - jnp.where(diagonal, 1.0, 0.0))
    turned = jnp.transpose(weights)
    img_along[...] = jnp.sum(weights * dots, axis=1, keepdims=True)
    txt_along[...] = jnp.sum(turned * jnp.transpose(dots), axis=1, keepdims=True)
    for grad, matrix, unit in ((img_grad, weights, txt_unit), (txt_grad, turned, img_unit)):
        high, low = halves(matrix)
        grad[...] = dot(jnp.concatenate([high, high], axis=1), unit[...], 0) + dot(low, unit[:rows, :], 0)


def guest_weights(scalars, unit, guest, along, stack, squares):
    rows = guest.shape[0]
    for start in range(0, rows, STRIP):
        values = guest[start : start + STRIP, :]
        high, low = halves(values)
        stack[start : start + STRIP, :] = high
        stack[rows + start : rows + start + STRIP, :] = low
        stack[2 * rows + start : 2 * rows + start + STRIP, :] = high
        total = jnp.sum(values * values, axis=-1, keepdims=True)
        squares[start : start + STRIP, :] = jnp.broadcast_to(total, (STRIP, squares.shape[1]))
    scale = scalars[0] / jnp.sqrt(jnp.transpose(squares[...])[0:1, :] + EPSILON)
    dots = row_dots(unit, stack, rows)
    weights = jax.nn.sigmoid(dots * scale + scalars[1]) * scale
    high, low = halves(weights)
    return along[...] + jnp.sum(weights * dots, axis=1, keepdims=True), jnp.concatenate([high, high, low], axis=1)


def guest_kernel(scalars, unit, guest, grad, along, grad_out, along_out, stack, squares):
    along_out[...], weights = guest_weights(scalars, unit, guest, along, stack, squares)
    grad_out[...] = grad[...] + dot(weights, stack[...], 0)


def last_kernel(scalars, unit, guest, grad, along, own, norm, out, stack, squares, result, sems):
    along, weights = guest_weights(scalars, unit, guest, along, stack, squares)
    inverse = 1.0 / norm[...]
    along = along * inverse * inverse
    copies = []
    for part in range(PARTS):
        width = out.shape[1] // PARTS
        span = slice(part * width, (part + 1) * width)
        result[:, span] = (grad[:, span] + dot(weights, stack[:, span], 0)) * inverse - own[:, span] * along
        copies.append(pltpu.make_async_copy(result.at[:, span], out.at[:, span], sems.at[part]))
        copies[-1].start()
    for copy in copies:
        copy.wait()


def call(kernel, outs, aliases, *operands, weight=FLOPS):
    rows, width = operands[2].shape
    in_specs = [pl.BlockSpec(memory_space=pltpu.SMEM)] + [pl.BlockSpec(memory_space=pltpu.VMEM)] * (len(operands) - 1)
    out_space, scratch = pltpu.VMEM, []
    if kernel is not own_kernel:
        scratch = [pltpu.VMEM((3 * rows, width), jnp.bfloat16), pltpu.VMEM((rows, 128), jnp.float32)]
    if kernel is last_kernel:
        out_space = pl.ANY
        scratch += [pltpu.VMEM(*outs[0]), pltpu.SemaphoreType.DMA((PARTS,))]
    return pl.pallas_call(
        kernel,
        out_shape=[jax.ShapeDtypeStruct(*out) for out in outs],
        in_specs=in_specs,
        out_specs=[pl.BlockSpec(memory_space=out_space)] * len(outs),
        scratch_shapes=scratch,
        input_output_aliases=aliases,
        cost_estimate=pl.CostEstimate(flops=weight * operands[1].size * rows, bytes_accessed=COST * rows, transcendentals=0),
        compiler_params=pltpu.CompilerParams(vmem_limit_bytes=VMEM_LIMIT),
    )(*operands)


def body(image_emb, text_emb, log_scale, logit_bias):
    scalars = jnp.concatenate([jnp.exp(log_scale), logit_bias])
    own = (image_emb, text_emb)
    out_far = [sent(value, outward, name) for value, name in zip(own, ("outward_image", "outward_text"))]
    in_far = [sent(image_emb, inward, "inward_image"), None]
    rows, width = image_emb.shape
    full, pair, column = ((rows, width), jnp.float32), ((2 * rows, width), jnp.bfloat16), ((rows, 1), jnp.float32)
    results = call(own_kernel, [pair] * 2 + [full] * 2 + [column] * 4, {}, scalars, *own, weight=0)
    units, grads, alongs, norms = results[0:2], list(results[2:4]), list(results[4:6]), results[6:8]

    def gated(*values):
        *values, grads[0], grads[1] = lax.optimization_barrier((*values, *grads))
        return values

    def add(kind, guest, weight=FLOPS):
        (guest,) = gated(guest)
        side = 1 - kind
        grads[side], alongs[side] = call(
            guest_kernel, [full, column], {3: 0, 4: 1}, scalars, units[side], guest, grads[side], alongs[side], weight=weight
        )

    def finish(kind, guest):
        (guest,) = gated(guest)
        side = 1 - kind
        return call(last_kernel, [full], {}, scalars, units[side], guest, grads[side], alongs[side], own[side], norms[side])[0]

    in_far[1] = sent(text_emb, inward, "inward_text")
    held = gated(*own)
    near = []
    for kind, name in ((0, "near_image"), (1, "near_text")):
        near += [(kind, sent(part, sibling, name)) for part in (held[kind][:NEAR_CUT], held[kind][NEAR_CUT:])]
    for kind, part in near:
        add(kind, part, 0)
    out_far[0], in_far[0] = gated(out_far[0], in_far[0])
    farthest = [sent(out_far[0], relay, "relay_image"), None]
    out_near = [sent(out_far[0], sibling, "outward_image_near"), None]
    in_near = [sent(in_far[0], sibling, "inward_image_near"), None]
    add(0, out_far[0])
    add(0, in_far[0])
    add(0, out_near[0])
    add(0, in_near[0])
    (out_far[1],) = gated(out_far[1])
    farthest[1] = [sent(part, relay, "relay_text") for part in (out_far[1][:CUT], out_far[1][CUT:])]
    out_near[1] = sent(out_far[1], sibling, "outward_text_near")
    add(1, out_far[1])
    add(1, out_near[1])
    (in_far[1],) = gated(in_far[1])
    in_near[1] = sent(in_far[1], sibling, "inward_text_near")
    add(1, in_far[1])
    add(1, in_near[1])
    text_grad = finish(0, farthest[0])
    part, text_grad = lax.optimization_barrier((farthest[1][0], text_grad))
    add(1, part)
    image_grad = finish(1, farthest[1][1])
    return image_grad, text_grad


def solution(mesh):
    placed = (P("batch", None), P("batch", None), P(), P())
    return jax.shard_map(
        body,
        mesh=mesh,
        in_specs=placed,
        out_specs=(P("batch", None), P("batch", None)),
        check_vma=False,
    )
```

```python
import functools

import jax
import jax.numpy as jnp
from jax import lax
from jax.experimental import pallas as pl
from jax.experimental.pallas import tpu as pltpu
from jax.sharding import PartitionSpec as P

EPSILON = 1e-06
FLOPS = 60
NEAR_CUT = 128
COST = 560000
CUT = 256
PARTS = 3
VMEM_LIMIT = 10 * 1024 * 1024
STRIP = 32


def outward(i):
    return i + 2 if i % 2 else i - 2


def inward(i):
    return i - 2 if i % 2 else i + 2


def relay(i):
    return i + 1 if i % 2 else i - 1


def sibling(i):
    return i ^ 1


def sent(value, where, name):
    count = lax.axis_size("batch")
    pairs = [(source, where(source) % count) for source in range(count)]
    with jax.named_scope(name):
        return lax.ppermute(value, "batch", pairs)


def halves(values):
    high = values.astype(jnp.bfloat16)
    return high, (values - high.astype(jnp.float32)).astype(jnp.bfloat16)


def dot(first, other, other_dim):
    return lax.dot_general(first, other, (((1,), (other_dim,)), ((), ())), preferred_element_type=jnp.float32)


def row_dots(unit, stack, rows):
    own = unit.shape[0] // 2
    wide = dot(unit[:own, :], stack[: 2 * rows, :], 1)
    return wide[:, :rows] + (wide[:, rows:] + dot(unit[own:, :], stack[:rows, :], 1))


def norm_of(values):
    return jnp.sqrt(jnp.sum(values * values, axis=-1, keepdims=True) + EPSILON)


def own_kernel(scalars, img, txt, img_unit, txt_unit, img_grad, txt_grad, img_along, txt_along, img_norm, txt_norm):
    temper, offset_bias = scalars[0], scalars[1]
    rows = img.shape[0]
    for source, unit, norms in ((img, img_unit, img_norm), (txt, txt_unit, txt_norm)):
        for start in range(0, rows, STRIP):
            values = source[start : start + STRIP, :]
            norm = norm_of(values)
            norms[start : start + STRIP, :] = norm
            unit[start : start + STRIP, :], unit[rows + start : rows + start + STRIP, :] = halves(values * (1.0 / norm))
    dots = row_dots(img_unit, txt_unit, rows)
    diagonal = lax.broadcasted_iota(jnp.int32, dots.shape, 0) == lax.broadcasted_iota(jnp.int32, dots.shape, 1)
    weights = temper * (jax.nn.sigmoid(temper * dots + offset_bias) - jnp.where(diagonal, 1.0, 0.0))
    turned = jnp.transpose(weights)
    img_along[...] = jnp.sum(weights * dots, axis=1, keepdims=True)
    txt_along[...] = jnp.sum(turned * jnp.transpose(dots), axis=1, keepdims=True)
    for grad, matrix, unit in ((img_grad, weights, txt_unit), (txt_grad, turned, img_unit)):
        high, low = halves(matrix)
        grad[...] = dot(jnp.concatenate([high, high], axis=1), unit[...], 0) + dot(low, unit[:rows, :], 0)


def guest_weights(scalars, unit, guest, along, stack, squares):
    rows = guest.shape[0]
    for start in range(0, rows, STRIP):
        values = guest[start : start + STRIP, :]
        high, low = halves(values)
        stack[start : start + STRIP, :] = high
        stack[rows + start : rows + start + STRIP, :] = low
        stack[2 * rows + start : 2 * rows + start + STRIP, :] = high
        total = jnp.sum(values * values, axis=-1, keepdims=True)
        squares[start : start + STRIP, :] = jnp.broadcast_to(total, (STRIP, squares.shape[1]))
    scale = scalars[0] / jnp.sqrt(jnp.transpose(squares[...])[0:1, :] + EPSILON)
    dots = row_dots(unit, stack, rows)
    weights = jax.nn.sigmoid(dots * scale + scalars[1]) * scale
    high, low = halves(weights)
    return along[...] + jnp.sum(weights * dots, axis=1, keepdims=True), jnp.concatenate([high, high, low], axis=1)


def guest_kernel(scalars, unit, guest, grad, along, grad_out, along_out, stack, squares):
    along_out[...], weights = guest_weights(scalars, unit, guest, along, stack, squares)
    width = grad.shape[1] // PARTS

    def block(index, carry):
        span = pl.ds(pl.multiple_of(index * width, width), width)
        grad_out[:, span] = grad[:, span] + dot(weights, stack[:, span], 0)
        return carry

    lax.fori_loop(0, PARTS, block, 0)


def last_kernel(scalars, unit, guest, grad, along, own, norm, out, stack, squares, result, sems):
    along, weights = guest_weights(scalars, unit, guest, along, stack, squares)
    inverse = 1.0 / norm[...]
    along = along * inverse * inverse
    copies = []
    for part in range(PARTS):
        width = out.shape[1] // PARTS
        span = slice(part * width, (part + 1) * width)
        result[:, span] = (grad[:, span] + dot(weights, stack[:, span], 0)) * inverse - own[:, span] * along
        copies.append(pltpu.make_async_copy(result.at[:, span], out.at[:, span], sems.at[part]))
        copies[-1].start()
    for copy in copies:
        copy.wait()


def call(kernel, outs, aliases, *operands, weight=FLOPS):
    rows, width = operands[2].shape
    in_specs = [pl.BlockSpec(memory_space=pltpu.SMEM)] + [pl.BlockSpec(memory_space=pltpu.VMEM)] * (len(operands) - 1)
    out_space, scratch = pltpu.VMEM, []
    if kernel is not own_kernel:
        scratch = [pltpu.VMEM((3 * rows, width), jnp.bfloat16), pltpu.VMEM((rows, 128), jnp.float32)]
    if kernel is last_kernel:
        out_space = pl.ANY
        scratch += [pltpu.VMEM(*outs[0]), pltpu.SemaphoreType.DMA((PARTS,))]
    return pl.pallas_call(
        kernel,
        out_shape=[jax.ShapeDtypeStruct(*out) for out in outs],
        in_specs=in_specs,
        out_specs=[pl.BlockSpec(memory_space=out_space)] * len(outs),
        scratch_shapes=scratch,
        input_output_aliases=aliases,
        cost_estimate=pl.CostEstimate(flops=weight * operands[1].size * rows, bytes_accessed=COST * rows, transcendentals=0),
        compiler_params=pltpu.CompilerParams(vmem_limit_bytes=VMEM_LIMIT),
    )(*operands)


def body(image_emb, text_emb, log_scale, logit_bias):
    scalars = jnp.concatenate([jnp.exp(log_scale), logit_bias])
    own = (image_emb, text_emb)
    out_far = [sent(value, outward, name) for value, name in zip(own, ("outward_image", "outward_text"))]
    in_far = [sent(image_emb, inward, "inward_image"), None]
    rows, width = image_emb.shape
    full, pair, column = ((rows, width), jnp.float32), ((2 * rows, width), jnp.bfloat16), ((rows, 1), jnp.float32)
    results = call(own_kernel, [pair] * 2 + [full] * 2 + [column] * 4, {}, scalars, *own, weight=0)
    units, grads, alongs, norms = results[0:2], list(results[2:4]), list(results[4:6]), results[6:8]

    def gated(*values):
        *values, grads[0], grads[1] = lax.optimization_barrier((*values, *grads))
        return values

    def add(kind, guest, weight=FLOPS):
        (guest,) = gated(guest)
        side = 1 - kind
        grads[side], alongs[side] = call(
            guest_kernel, [full, column], {3: 0, 4: 1}, scalars, units[side], guest, grads[side], alongs[side], weight=weight
        )

    def finish(kind, guest):
        (guest,) = gated(guest)
        side = 1 - kind
        return call(last_kernel, [full], {}, scalars, units[side], guest, grads[side], alongs[side], own[side], norms[side])[0]

    in_far[1] = sent(text_emb, inward, "inward_text")
    held = gated(*own)
    near = []
    for kind, name in ((0, "near_image"), (1, "near_text")):
        near += [(kind, sent(part, sibling, name)) for part in (held[kind][:NEAR_CUT], held[kind][NEAR_CUT:])]
    for kind, part in near:
        add(kind, part, 0)
    out_far[0], in_far[0] = gated(out_far[0], in_far[0])
    farthest = [sent(out_far[0], relay, "relay_image"), None]
    out_near = [sent(out_far[0], sibling, "outward_image_near"), None]
    in_near = [sent(in_far[0], sibling, "inward_image_near"), None]
    add(0, out_far[0])
    add(0, in_far[0])
    add(0, out_near[0])
    add(0, in_near[0])
    (out_far[1],) = gated(out_far[1])
    farthest[1] = [sent(part, relay, "relay_text") for part in (out_far[1][:CUT], out_far[1][CUT:])]
    out_near[1] = sent(out_far[1], sibling, "outward_text_near")
    add(1, out_far[1])
    add(1, out_near[1])
    (in_far[1],) = gated(in_far[1])
    in_near[1] = sent(in_far[1], sibling, "inward_text_near")
    add(1, in_far[1])
    add(1, in_near[1])
    text_grad = finish(0, farthest[0])
    part, text_grad = lax.optimization_barrier((farthest[1][0], text_grad))
    add(1, part)
    image_grad = finish(1, farthest[1][1])
    return image_grad, text_grad


def solution(mesh):
    placed = (P("batch", None), P("batch", None), P(), P())
    return jax.shard_map(
        body,
        mesh=mesh,
        in_specs=placed,
        out_specs=(P("batch", None), P("batch", None)),
        check_vma=False,
    )
```

```python
import functools

import jax
import jax.numpy as jnp
from jax import lax
from jax.experimental import pallas as pl
from jax.experimental.pallas import tpu as pltpu
from jax.sharding import PartitionSpec as P

EPSILON = 1e-06
FLOPS = 60
NEAR_CUT = 128
COST = 560000
CUT = 256
PARTS = 3
VMEM_LIMIT = 10 * 1024 * 1024
STRIP = 32


def outward(i):
    return i + 2 if i % 2 else i - 2


def inward(i):
    return i - 2 if i % 2 else i + 2


def relay(i):
    return i + 1 if i % 2 else i - 1


def sibling(i):
    return i ^ 1


def sent(value, where, name):
    count = lax.axis_size("batch")
    pairs = [(source, where(source) % count) for source in range(count)]
    with jax.named_scope(name):
        return lax.ppermute(value, "batch", pairs)


def halves(values):
    high = values.astype(jnp.bfloat16)
    return high, (values - high.astype(jnp.float32)).astype(jnp.bfloat16)


def dot(first, other, other_dim):
    return lax.dot_general(first, other, (((1,), (other_dim,)), ((), ())), preferred_element_type=jnp.float32)


def row_dots(unit, stack, rows):
    own = unit.shape[0] // 2
    wide = dot(unit[:own, :], stack[: 2 * rows, :], 1)
    return wide[:, :rows] + (wide[:, rows:] + dot(unit[own:, :], stack[:rows, :], 1))


def norm_of(values):
    return jnp.sqrt(jnp.sum(values * values, axis=-1, keepdims=True) + EPSILON)


def own_kernel(scalars, img, txt, img_unit, txt_unit, img_grad, txt_grad, img_along, txt_along, img_norm, txt_norm):
    temper, offset_bias = scalars[0], scalars[1]
    rows = img.shape[0]
    for source, unit, norms in ((img, img_unit, img_norm), (txt, txt_unit, txt_norm)):
        for start in range(0, rows, STRIP):
            values = source[start : start + STRIP, :]
            norm = norm_of(values)
            norms[start : start + STRIP, :] = norm
            unit[start : start + STRIP, :], unit[rows + start : rows + start + STRIP, :] = halves(values * (1.0 / norm))
    dots = row_dots(img_unit, txt_unit, rows)
    diagonal = lax.broadcasted_iota(jnp.int32, dots.shape, 0) == lax.broadcasted_iota(jnp.int32, dots.shape, 1)
    weights = temper * (jax.nn.sigmoid(temper * dots + offset_bias) - jnp.where(diagonal, 1.0, 0.0))
    turned = jnp.transpose(weights)
    img_along[...] = jnp.sum(weights * dots, axis=1, keepdims=True)
    txt_along[...] = jnp.sum(turned * jnp.transpose(dots), axis=1, keepdims=True)
    for grad, matrix, unit in ((img_grad, weights, txt_unit), (txt_grad, turned, img_unit)):
        high, low = halves(matrix)
        grad[...] = dot(jnp.concatenate([high, high], axis=1), unit[...], 0) + dot(low, unit[:rows, :], 0)


def guest_weights(scalars, unit, guest, along, stack, squares):
    rows = guest.shape[0]
    for start in range(0, rows, STRIP):
        values = guest[start : start + STRIP, :]
        high, low = halves(values)
        stack[start : start + STRIP, :] = high
        stack[rows + start : rows + start + STRIP, :] = low
        stack[2 * rows + start : 2 * rows + start + STRIP, :] = high
        total = jnp.sum(values * values, axis=-1, keepdims=True)
        squares[start : start + STRIP, :] = jnp.broadcast_to(total, (STRIP, squares.shape[1]))
    scale = scalars[0] / jnp.sqrt(jnp.transpose(squares[...])[0:1, :] + EPSILON)
    dots = row_dots(unit, stack, rows)
    weights = jax.nn.sigmoid(dots * scale + scalars[1]) * scale
    high, low = halves(weights)
    return along[...] + jnp.sum(weights * dots, axis=1, keepdims=True), jnp.concatenate([high, high, low], axis=1)


def guest_kernel(scalars, unit, guest, grad, along, grad_out, along_out, stack, squares):
    along_out[...], weights = guest_weights(scalars, unit, guest, along, stack, squares)
    if guest.shape[0] == unit.shape[0] // 2:
        grad_out[...] = grad[...] + dot(weights, stack[...], 0)
        return
    width = grad.shape[1] // PARTS

    def block(index, carry):
        span = pl.ds(pl.multiple_of(index * width, width), width)
        grad_out[:, span] = grad[:, span] + dot(weights, stack[:, span], 0)
        return carry

    lax.fori_loop(0, PARTS, block, 0)


def last_kernel(scalars, unit, guest, grad, along, own, norm, out, stack, squares, result, sems):
    along, weights = guest_weights(scalars, unit, guest, along, stack, squares)
    inverse = 1.0 / norm[...]
    along = along * inverse * inverse
    copies = []
    for part in range(PARTS):
        width = out.shape[1] // PARTS
        span = slice(part * width, (part + 1) * width)
        result[:, span] = (grad[:, span] + dot(weights, stack[:, span], 0)) * inverse - own[:, span] * along
        copies.append(pltpu.make_async_copy(result.at[:, span], out.at[:, span], sems.at[part]))
        copies[-1].start()
    for copy in copies:
        copy.wait()


def call(kernel, outs, aliases, *operands, weight=FLOPS):
    rows, width = operands[2].shape
    in_specs = [pl.BlockSpec(memory_space=pltpu.SMEM)] + [pl.BlockSpec(memory_space=pltpu.VMEM)] * (len(operands) - 1)
    out_space, scratch = pltpu.VMEM, []
    if kernel is not own_kernel:
        scratch = [pltpu.VMEM((3 * rows, width), jnp.bfloat16), pltpu.VMEM((rows, 128), jnp.float32)]
    if kernel is last_kernel:
        out_space = pl.ANY
        scratch += [pltpu.VMEM(*outs[0]), pltpu.SemaphoreType.DMA((PARTS,))]
    return pl.pallas_call(
        kernel,
        out_shape=[jax.ShapeDtypeStruct(*out) for out in outs],
        in_specs=in_specs,
        out_specs=[pl.BlockSpec(memory_space=out_space)] * len(outs),
        scratch_shapes=scratch,
        input_output_aliases=aliases,
        cost_estimate=pl.CostEstimate(flops=weight * operands[1].size * rows, bytes_accessed=COST * rows, transcendentals=0),
        compiler_params=pltpu.CompilerParams(vmem_limit_bytes=VMEM_LIMIT),
    )(*operands)


def body(image_emb, text_emb, log_scale, logit_bias):
    scalars = jnp.concatenate([jnp.exp(log_scale), logit_bias])
    own = (image_emb, text_emb)
    out_far = [sent(value, outward, name) for value, name in zip(own, ("outward_image", "outward_text"))]
    in_far = [sent(image_emb, inward, "inward_image"), None]
    rows, width = image_emb.shape
    full, pair, column = ((rows, width), jnp.float32), ((2 * rows, width), jnp.bfloat16), ((rows, 1), jnp.float32)
    results = call(own_kernel, [pair] * 2 + [full] * 2 + [column] * 4, {}, scalars, *own, weight=0)
    units, grads, alongs, norms = results[0:2], list(results[2:4]), list(results[4:6]), results[6:8]

    def gated(*values):
        *values, grads[0], grads[1] = lax.optimization_barrier((*values, *grads))
        return values

    def add(kind, guest, weight=FLOPS):
        (guest,) = gated(guest)
        side = 1 - kind
        grads[side], alongs[side] = call(
            guest_kernel, [full, column], {3: 0, 4: 1}, scalars, units[side], guest, grads[side], alongs[side], weight=weight
        )

    def finish(kind, guest):
        (guest,) = gated(guest)
        side = 1 - kind
        return call(last_kernel, [full], {}, scalars, units[side], guest, grads[side], alongs[side], own[side], norms[side])[0]

    in_far[1] = sent(text_emb, inward, "inward_text")
    held = gated(*own)
    near = []
    for kind, name in ((0, "near_image"), (1, "near_text")):
        near += [(kind, sent(part, sibling, name)) for part in (held[kind][:NEAR_CUT], held[kind][NEAR_CUT:])]
    for kind, part in near:
        add(kind, part, 0)
    out_far[0], in_far[0] = gated(out_far[0], in_far[0])
    farthest = [sent(out_far[0], relay, "relay_image"), None]
    out_near = [sent(out_far[0], sibling, "outward_image_near"), None]
    in_near = [sent(in_far[0], sibling, "inward_image_near"), None]
    add(0, out_far[0])
    add(0, in_far[0])
    add(0, out_near[0])
    add(0, in_near[0])
    (out_far[1],) = gated(out_far[1])
    farthest[1] = [sent(part, relay, "relay_text") for part in (out_far[1][:CUT], out_far[1][CUT:])]
    out_near[1] = sent(out_far[1], sibling, "outward_text_near")
    add(1, out_far[1])
    add(1, out_near[1])
    (in_far[1],) = gated(in_far[1])
    in_near[1] = sent(in_far[1], sibling, "inward_text_near")
    add(1, in_far[1])
    add(1, in_near[1])
    text_grad = finish(0, farthest[0])
    part, text_grad = lax.optimization_barrier((farthest[1][0], text_grad))
    add(1, part)
    image_grad = finish(1, farthest[1][1])
    return image_grad, text_grad


def solution(mesh):
    placed = (P("batch", None), P("batch", None), P(), P())
    return jax.shard_map(
        body,
        mesh=mesh,
        in_specs=placed,
        out_specs=(P("batch", None), P("batch", None)),
        check_vma=False,
    )
```

```python
import functools

import jax
import jax.numpy as jnp
from jax import lax
from jax.experimental import pallas as pl
from jax.experimental.pallas import tpu as pltpu
from jax.sharding import PartitionSpec as P

EPSILON = 1e-06
FLOPS = 60
NEAR_CUT = 128
COST = 560000
CUT = 256
PARTS = 3
VMEM_LIMIT = 10 * 1024 * 1024
STRIP = 32


def outward(i):
    return i + 2 if i % 2 else i - 2


def inward(i):
    return i - 2 if i % 2 else i + 2


def relay(i):
    return i + 1 if i % 2 else i - 1


def sibling(i):
    return i ^ 1


def sent(value, where, name):
    count = lax.axis_size("batch")
    pairs = [(source, where(source) % count) for source in range(count)]
    with jax.named_scope(name):
        return lax.ppermute(value, "batch", pairs)


def halves(values):
    high = values.astype(jnp.bfloat16)
    return high, (values - high.astype(jnp.float32)).astype(jnp.bfloat16)


def dot(first, other, other_dim):
    return lax.dot_general(first, other, (((1,), (other_dim,)), ((), ())), preferred_element_type=jnp.float32)


def row_dots(unit, stack, rows):
    own = unit.shape[0] // 2
    wide = dot(unit[:own, :], stack[: 2 * rows, :], 1)
    return wide[:, :rows] + (wide[:, rows:] + dot(unit[own:, :], stack[:rows, :], 1))


def norm_of(values):
    return jnp.sqrt(jnp.sum(values * values, axis=-1, keepdims=True) + EPSILON)


def own_kernel(scalars, img, txt, img_unit, txt_unit, img_grad, txt_grad, img_along, txt_along, img_norm, txt_norm):
    temper, offset_bias = scalars[0], scalars[1]
    rows = img.shape[0]
    for source, unit, norms in ((img, img_unit, img_norm), (txt, txt_unit, txt_norm)):
        for start in range(0, rows, STRIP):
            values = source[start : start + STRIP, :]
            norm = norm_of(values)
            norms[start : start + STRIP, :] = norm
            unit[start : start + STRIP, :], unit[rows + start : rows + start + STRIP, :] = halves(values * (1.0 / norm))
    dots = row_dots(img_unit, txt_unit, rows)
    diagonal = lax.broadcasted_iota(jnp.int32, dots.shape, 0) == lax.broadcasted_iota(jnp.int32, dots.shape, 1)
    weights = temper * (jax.nn.sigmoid(temper * dots + offset_bias) - jnp.where(diagonal, 1.0, 0.0))
    turned = jnp.transpose(weights)
    img_along[...] = jnp.sum(weights * dots, axis=1, keepdims=True)
    txt_along[...] = jnp.sum(turned * jnp.transpose(dots), axis=1, keepdims=True)
    for grad, matrix, unit in ((img_grad, weights, txt_unit), (txt_grad, turned, img_unit)):
        high, low = halves(matrix)
        grad[...] = dot(jnp.concatenate([high, high], axis=1), unit[...], 0) + dot(low, unit[:rows, :], 0)


def guest_weights(scalars, unit, guests, along, stack, squares):
    rows = sum(guest.shape[0] for guest in guests)
    strips = [(guest, begin) for guest in guests for begin in range(0, guest.shape[0], STRIP)]
    for index, (guest, begin) in enumerate(strips):
        start = index * STRIP
        values = guest[begin : begin + STRIP, :]
        high, low = halves(values)
        stack[start : start + STRIP, :] = high
        stack[rows + start : rows + start + STRIP, :] = low
        stack[2 * rows + start : 2 * rows + start + STRIP, :] = high
        total = jnp.sum(values * values, axis=-1, keepdims=True)
        squares[start : start + STRIP, :] = jnp.broadcast_to(total, (STRIP, squares.shape[1]))
    scale = scalars[0] / jnp.sqrt(jnp.transpose(squares[...])[0:1, :] + EPSILON)
    dots = row_dots(unit, stack, rows)
    weights = jax.nn.sigmoid(dots * scale + scalars[1]) * scale
    high, low = halves(weights)
    return along[...] + jnp.sum(weights * dots, axis=1, keepdims=True), jnp.concatenate([high, high, low], axis=1)


def guest_kernel(scalars, unit, guest, grad, along, grad_out, along_out, stack, squares):
    along_out[...], weights = guest_weights(scalars, unit, (guest,), along, stack, squares)
    grad_out[...] = grad[...] + dot(weights, stack[...], 0)


def pieces_kernel(scalars, unit, first, second, grad, along, grad_out, along_out, stack, squares):
    along_out[...], weights = guest_weights(scalars, unit, (first, second), along, stack, squares)
    grad_out[...] = grad[...] + dot(weights, stack[...], 0)


def last_kernel(scalars, unit, guest, grad, along, own, norm, out, stack, squares, result, sems):
    along, weights = guest_weights(scalars, unit, (guest,), along, stack, squares)
    inverse = 1.0 / norm[...]
    along = along * inverse * inverse
    copies = []
    for part in range(PARTS):
        width = out.shape[1] // PARTS
        span = slice(part * width, (part + 1) * width)
        result[:, span] = (grad[:, span] + dot(weights, stack[:, span], 0)) * inverse - own[:, span] * along
        copies.append(pltpu.make_async_copy(result.at[:, span], out.at[:, span], sems.at[part]))
        copies[-1].start()
    for copy in copies:
        copy.wait()


def call(kernel, outs, aliases, *operands, weight=FLOPS):
    rows, width = operands[2].shape
    if kernel is pieces_kernel:
        rows += operands[3].shape[0]
    in_specs = [pl.BlockSpec(memory_space=pltpu.SMEM)] + [pl.BlockSpec(memory_space=pltpu.VMEM)] * (len(operands) - 1)
    out_space, scratch = pltpu.VMEM, []
    if kernel is not own_kernel:
        scratch = [pltpu.VMEM((3 * rows, width), jnp.bfloat16), pltpu.VMEM((rows, 128), jnp.float32)]
    if kernel is last_kernel:
        out_space = pl.ANY
        scratch += [pltpu.VMEM(*outs[0]), pltpu.SemaphoreType.DMA((PARTS,))]
    return pl.pallas_call(
        kernel,
        out_shape=[jax.ShapeDtypeStruct(*out) for out in outs],
        in_specs=in_specs,
        out_specs=[pl.BlockSpec(memory_space=out_space)] * len(outs),
        scratch_shapes=scratch,
        input_output_aliases=aliases,
        cost_estimate=pl.CostEstimate(flops=weight * operands[1].size * rows, bytes_accessed=COST * rows, transcendentals=0),
        compiler_params=pltpu.CompilerParams(vmem_limit_bytes=VMEM_LIMIT),
    )(*operands)


def body(image_emb, text_emb, log_scale, logit_bias):
    scalars = jnp.concatenate([jnp.exp(log_scale), logit_bias])
    own = (image_emb, text_emb)
    out_far = [sent(value, outward, name) for value, name in zip(own, ("outward_image", "outward_text"))]
    in_far = [sent(image_emb, inward, "inward_image"), None]
    rows, width = image_emb.shape
    full, pair, column = ((rows, width), jnp.float32), ((2 * rows, width), jnp.bfloat16), ((rows, 1), jnp.float32)
    results = call(own_kernel, [pair] * 2 + [full] * 2 + [column] * 4, {}, scalars, *own, weight=0)
    units, grads, alongs, norms = results[0:2], list(results[2:4]), list(results[4:6]), results[6:8]

    def gated(*values):
        *values, grads[0], grads[1] = lax.optimization_barrier((*values, *grads))
        return values

    def add(kind, guest, weight=FLOPS):
        (guest,) = gated(guest)
        side = 1 - kind
        grads[side], alongs[side] = call(
            guest_kernel, [full, column], {3: 0, 4: 1}, scalars, units[side], guest, grads[side], alongs[side], weight=weight
        )

    def finish(kind, guest):
        (guest,) = gated(guest)
        side = 1 - kind
        return call(last_kernel, [full], {}, scalars, units[side], guest, grads[side], alongs[side], own[side], norms[side])[0]

    in_far[1] = sent(text_emb, inward, "inward_text")
    held = gated(*own)
    near = []
    for kind, name in ((0, "near_image"), (1, "near_text")):
        near.append([sent(part, sibling, name) for part in (held[kind][:NEAR_CUT], held[kind][NEAR_CUT:])])
    for kind in (0, 1):
        side = 1 - kind
        first, second = gated(*near[kind])
        grads[side], alongs[side] = call(
            pieces_kernel, [full, column], {4: 0, 5: 1}, scalars, units[side], first, second, grads[side], alongs[side], weight=0
        )
    out_far[0], in_far[0] = gated(out_far[0], in_far[0])
    farthest = [sent(out_far[0], relay, "relay_image"), None]
    out_near = [sent(out_far[0], sibling, "outward_image_near"), None]
    in_near = [sent(in_far[0], sibling, "inward_image_near"), None]
    add(0, out_far[0])
    add(0, in_far[0])
    add(0, out_near[0])
    add(0, in_near[0])
    (out_far[1],) = gated(out_far[1])
    farthest[1] = [sent(part, relay, "relay_text") for part in (out_far[1][:CUT], out_far[1][CUT:])]
    out_near[1] = sent(out_far[1], sibling, "outward_text_near")
    add(1, out_far[1])
    add(1, out_near[1])
    (in_far[1],) = gated(in_far[1])
    in_near[1] = sent(in_far[1], sibling, "inward_text_near")
    add(1, in_far[1])
    add(1, in_near[1])
    text_grad = finish(0, farthest[0])
    part, text_grad = lax.optimization_barrier((farthest[1][0], text_grad))
    add(1, part)
    image_grad = finish(1, farthest[1][1])
    return image_grad, text_grad


def solution(mesh):
    placed = (P("batch", None), P("batch", None), P(), P())
    return jax.shard_map(
        body,
        mesh=mesh,
        in_specs=placed,
        out_specs=(P("batch", None), P("batch", None)),
        check_vma=False,
    )
```
